256 devices in a mesh: ctx: 8 (over y, core), tp: 8 (over z), vocab: 4 (over x).
Axes of the slice: x: 4, y: 4, z: 8, core: 2. Of those that a mesh axis runs over, the one named last changes fastest.
Arguments:
- lengths: int32 [8], replicated, may hold values from 4096 to 16384, as said below
- queries: bfloat16 [8, 16384], P(None, 'tp'), may hold values from -15 to 15
- cache_keys: bfloat16 [8, 16384, 1024], P(None, ('ctx', 'vocab'), 'tp'), may hold values from -6 to 6
- cache_values: bfloat16 [8, 16384, 1024], P(None, ('ctx', 'vocab'), 'tp'), may hold values from -6 to 6
- out_weight: bfloat16 [16384, 16384], P('tp', ('ctx', 'vocab')), may hold values from -0.09375 to 0.09375
- residual: bfloat16 [8, 16384], P(None, ('ctx', 'vocab')), may hold values from -6 to 6
- norm_gain: float32 [16384], P(('ctx', 'vocab')), may hold values from 0.5 to 1.5
- head_weight: bfloat16 [16384, 65536], P(('ctx', 'vocab'), 'tp'), may hold values from -0.25 to 0.25
Outputs:
- log_probs: float32 [8, 65536], P(None, 'tp')
The draws below stay inside these ranges and needn't reach their ends.
Inputs may be any that keep to these rules, and one draw needn't show every extreme that they name: `lengths`: in every draw one row has length exactly 16384.
All inputs are finite; a program needn't handle non-finite values.
Results may differ from the reference program's by a relative error of at most 0.0025.
Values sent between devices are 32-bit elements; how exact they have to be, the bound alone decides.
A program may use at most 64 MiB of HBM per device.

```python
import math
import jax
import jax.numpy as jnp
from jax import lax

B = 8
D = 16384
QH = 128
KVH = 8
HD = 128
V = 65536
LENGTH = 16384


def draw_lengths(key, part):
    key = jax.random.fold_in(key, 5)
    first_key, second_key = jax.random.split(key)
    drawn = jax.random.randint(first_key, (B,), LENGTH // 4, LENGTH + 1)
    longest = jax.random.randint(second_key, (), 0, B)
    return jnp.where(jnp.arange(B) == longest, LENGTH, drawn).astype(jnp.int32)


def draw_queries(key, part):
    key = jax.random.fold_in(key, 11)
    values_drawn = 2.5 * jnp.clip(jax.random.normal(key, (B, QH, HD), jnp.float32), -6.0, 6.0)
    return values_drawn.reshape(B, QH * HD).astype(jnp.bfloat16)


def draw_cache_keys(key, part):
    key = jax.random.fold_in(key, 12)
    values_drawn = jnp.clip(jax.random.normal(key, (B, LENGTH, KVH, HD), jnp.float32), -6.0, 6.0)
    return values_drawn.reshape(B, LENGTH, KVH * HD).astype(jnp.bfloat16)


def draw_residual(key, part):
    key = jax.random.fold_in(key, 13)
    second_key = jax.random.fold_in(key, 1)
    feature = jnp.arange(D, dtype=jnp.float32) / D
    column_scale = 0.5 * jnp.sqrt(1.0 + 2.0 * feature)
    values_drawn = jnp.clip(jax.random.normal(second_key, (B, D), jnp.float32), -6.0, 6.0) * column_scale[None, :]
    return jnp.clip(values_drawn, -6.0, 6.0).astype(jnp.bfloat16)


def draw_head_weight(key, part):
    key = jax.random.fold_in(key, 14)
    spread = 3.0 / math.sqrt(D)
    values_drawn = spread * jnp.clip(jax.random.normal(key, (D, V), jnp.float32), -4.0, 4.0)
    return jnp.clip(values_drawn, -0.25, 0.25).astype(jnp.bfloat16)


def levels(own_key, dims, cuts, smallest, largest):
    gain = 1.0
    for dim, parts in cuts:
        draws = jax.random.uniform(jax.random.fold_in(jax.random.fold_in(own_key, 6), dim), (parts,), jnp.float32, smallest / len(cuts), largest / len(cuts))
        gain = gain * jnp.repeat(jnp.exp(draws), dims[dim] // parts).reshape((-1,) + (1,) * (len(dims) - 1 - dim))
    return gain


def centred(rng, dims, deviation, bound, pieces=(), held_as=jnp.bfloat16):
    level = levels(rng, dims, pieces, -0.22, 0.18) if pieces else 1.0
    values = jax.random.normal(rng, dims, jnp.float32) * deviation * level
    return jnp.minimum(jnp.maximum(values, -bound), bound).astype(held_as)


def setup_inputs(seed: int = 0) -> dict:
    streams_of = jax.random.split(jax.random.key(seed), 9)
    lengths = draw_lengths(jax.random.fold_in(streams_of[8], 71), 0)
    queries = draw_queries(jax.random.fold_in(streams_of[8], 71), 0)
    cache_keys = draw_cache_keys(jax.random.fold_in(streams_of[8], 71), 0)
    cache_values = centred(streams_of[3], (B, LENGTH, KVH * HD), 1.0, 6.0, ((1, 32), (2, 8)))
    out_weight = centred(streams_of[4], (QH * HD, D), (QH * HD // 4) ** -0.5, 0.09375, ((0, 8), (1, 32)))
    residual = draw_residual(jax.random.fold_in(streams_of[8], 71), 0)
    norm_gain = jnp.clip(1.0 + 0.1 * jax.random.normal(streams_of[6], (D,), jnp.float32), 0.5, 1.5)
    head_weight = draw_head_weight(jax.random.fold_in(streams_of[8], 71), 0)
    return dict(lengths=lengths, queries=queries, cache_keys=cache_keys, cache_values=cache_values, out_weight=out_weight, residual=residual, norm_gain=norm_gain, head_weight=head_weight)


def attend_row(row_item):
    query_row, key_rows, value_rows, row_length = row_item
    group_size = QH // KVH
    query_heads = query_row.reshape(KVH, group_size, HD).astype(jnp.float32)
    key_heads = key_rows.reshape(LENGTH, KVH, HD).astype(jnp.float32)
    value_heads = value_rows.reshape(LENGTH, KVH, HD).astype(jnp.float32)
    scores = jnp.einsum('kgd,ckd->kgc', query_heads, key_heads) * HD ** (-0.5)
    valid = jnp.arange(LENGTH, dtype=jnp.int32) < row_length
    masked = jnp.where(valid, scores, -1e+30)
    peak_value = lax.optimization_barrier(jnp.max(masked, axis=2, keepdims=True))
    expo = jnp.where(valid, jnp.exp(masked - peak_value), 0.0)
    totals = lax.optimization_barrier(jnp.sum(expo, axis=2))
    weights = lax.optimization_barrier(expo.astype(jnp.bfloat16)).astype(jnp.float32)
    mixed = jnp.einsum('kgc,ckd->kgd', weights, value_heads)
    return (mixed / totals[:, :, None]).astype(jnp.bfloat16).reshape(QH * HD)

def reference(lengths, queries, cache_keys, cache_values, out_weight, residual, norm_gain, head_weight):
    attended = lax.map(attend_row, (queries, cache_keys, cache_values, lengths))
    hidden = residual.astype(jnp.float32) + jnp.dot(attended, out_weight, preferred_element_type=jnp.float32)
    mean_square = lax.optimization_barrier(jnp.sum(hidden * hidden, axis=1)) / D
    normed = (hidden * lax.rsqrt(mean_square + 1e-05)[:, None] * norm_gain).astype(jnp.bfloat16)
    logits = jnp.dot(normed, head_weight, preferred_element_type=jnp.float32)
    peak_logit = lax.optimization_barrier(jnp.max(logits, axis=1, keepdims=True))
    log_total = jnp.log(lax.optimization_barrier(jnp.sum(jnp.exp(logits - peak_logit), axis=1, keepdims=True)))
    return logits - peak_logit - log_total
```

```python
import functools

import jax
import jax.numpy as jnp
from jax import lax
from jax.experimental import pallas as pl
from jax.experimental.pallas import tpu as pltpu
from jax.sharding import PartitionSpec as P

MESH = pl.DeviceIdType.MESH
B = 8
D = 16384
HD = 128
GROUP = 16
CTX, TP, VOCAB = 8, 8, 4
PLANE = CTX * VOCAB
SLOTS = 512
FEAT = 512
VSLICE = 256
F32 = jnp.float32
BF16 = jnp.bfloat16


def kernel(
    len_hbm, q_hbm, k_hbm, v_hbm, w_hbm, res_hbm, gain_hbm, head_hbm,
    out_ref,
    lens, q, k, v, w, res, gain, head, qs,
    part, parts, att, proj, terms, gathered, fin, zstat, pstat,
    load_sem, send_sem, recv_sem,
):
    ctx, tp, voc = lax.axis_index("ctx"), lax.axis_index("tp"), lax.axis_index("vocab")
    me = ctx * VOCAB + voc

    loads = [
        pltpu.make_async_copy(src, dst, load_sem.at[i])
        for i, (src, dst) in enumerate(
            [(q_hbm, q), (len_hbm, lens), (k_hbm, k), (v_hbm, v), (w_hbm, w), (res_hbm, res), (gain_hbm, gain), (head_hbm, head)]
        )
    ]
    for load in loads:
        load.start()

    def plane_peer(step):
        c = lax.rem(ctx + step // VOCAB, CTX)
        x = lax.rem(voc + lax.rem(step, VOCAB), VOCAB)
        return c * VOCAB + x, (c, tp, x)

    def z_peer(step):
        return (ctx, lax.rem(tp + step, TP), voc)

    barrier = pltpu.get_barrier_semaphore()

    def greet_plane(step, carry):
        pl.semaphore_signal(barrier, inc=1, device_id=plane_peer(step)[1], device_id_type=MESH)
        return carry

    def greet_z(step, carry):
        pl.semaphore_signal(barrier, inc=1, device_id=z_peer(step), device_id_type=MESH)
        return carry

    lax.fori_loop(1, PLANE, greet_plane, 0)
    lax.fori_loop(1, TP, greet_z, 0)

    def send(stage, src, dst, device):
        pltpu.make_async_remote_copy(
            src_ref=src, dst_ref=dst, send_sem=send_sem.at[stage], recv_sem=recv_sem.at[stage],
            device_id=device, device_id_type=MESH,
        ).start()

    def await_bytes(sem, like):
        pltpu.make_async_copy(like, like, sem).wait()

    loads[0].wait()
    for h in range(GROUP):
        qs[pl.ds(h * B, B), :] = q[:, h * HD : (h + 1) * HD].astype(F32)
    loads[1].wait()
    loads[2].wait()
    loads[3].wait()
    position = me * SLOTS + lax.broadcasted_iota(jnp.int32, (GROUP, SLOTS), 1)
    lane = lax.broadcasted_iota(jnp.int32, (GROUP, HD), 1)
    for b in range(B):
        query = qs[pl.ds(b, GROUP, stride=B), :].astype(BF16)
        scores = lax.dot_general(query, k[b], (((1,), (1,)), ((), ())), preferred_element_type=F32) * HD ** (-0.5)
        valid = position < lens[b]
        masked = jnp.where(valid, scores, -1e30)
        peak = jnp.max(masked, axis=1, keepdims=True)
        expo = jnp.where(valid, jnp.exp(masked - peak), 0.0)
        total = jnp.sum(expo, axis=1, keepdims=True)
        mixed = jnp.dot(expo.astype(BF16), v[b], preferred_element_type=F32)
        row = (b // 4) * 8 + b % 4
        part[pl.ds(row, GROUP, stride=16), :] = mixed
        part[pl.ds(row + 4, GROUP, stride=16), :] = jnp.where(lane < 64, peak, total)

    pl.semaphore_wait(barrier, PLANE - 1 + TP - 1)

    def scatter_part(step, carry):
        slot, device = plane_peer(step)
        send(0, part.at[pl.ds(pl.multiple_of(slot * 8, 8), 8), :], parts.at[me], device)
        return carry

    lax.fori_loop(1, PLANE, scatter_part, 0)
    parts[me] = part[pl.ds(pl.multiple_of(me * 8, 8), 8), :]
    await_bytes(recv_sem.at[0], parts.at[pl.ds(0, PLANE - 1)])
    stats = parts[:, 4:8, :]
    swapped = pltpu.roll(stats.reshape(PLANE * 4, HD), 64, 1).reshape(PLANE, 4, HD)
    low = lax.broadcasted_iota(jnp.int32, (PLANE, 4, HD), 2) < 64
    peaks = jnp.where(low, stats, swapped)
    totals = jnp.where(low, swapped, stats)
    top = jnp.max(peaks, axis=0, keepdims=True)
    factor = jnp.exp(peaks - top)
    total = jnp.sum(totals * factor, axis=0)
    attended = jnp.sum(parts[:, 0:4, :] * factor, axis=0) / total
    att[me] = attended

    def gather_att(step, carry):
        send(1, att.at[me], att.at[me], plane_peer(step)[1])
        return carry

    lax.fori_loop(1, PLANE, gather_att, 0)
    loads[4].wait()
    await_bytes(recv_sem.at[1], att.at[pl.ds(0, PLANE - 1)])
    heads = [
        jnp.concatenate([att[2 * h], att[2 * h + 1]], axis=0).astype(BF16) for h in range(GROUP)
    ]
    proj[tp] = jnp.dot(jnp.concatenate(heads, axis=1), w[...], preferred_element_type=F32)

    def gather_proj(step, carry):
        send(2, proj.at[tp], proj.at[tp], z_peer(step))
        return carry

    lax.fori_loop(1, TP, gather_proj, 0)
    loads[5].wait()
    loads[6].wait()
    loads[7].wait()
    await_bytes(recv_sem.at[2], proj.at[pl.ds(0, TP - 1)])
    hidden = res[...].astype(F32) + jnp.sum(proj[...], axis=0)
    diagonal = lax.broadcasted_iota(jnp.int32, (B, HD), 0) == lax.broadcasted_iota(jnp.int32, (B, HD), 1)
    squares = jnp.sum(hidden * hidden, axis=1, keepdims=True)
    square_row = jnp.sum(jnp.where(diagonal, squares, 0.0), axis=0, keepdims=True)
    scaled = (hidden * gain[...].reshape(1, FEAT)).astype(BF16)

    def head_block(step, carry):
        c = lax.rem(ctx + step, CTX)
        width = VOCAB * VSLICE
        columns = pl.ds(pl.multiple_of(c * width, width), width)
        block = jnp.dot(scaled, head[:, columns], preferred_element_type=F32)
        for x in range(VOCAB):
            slot = c * VOCAB + x
            terms[slot, 0:8, :] = block[:, x * VSLICE : x * VSLICE + HD]
            terms[slot, 8:16, :] = block[:, x * VSLICE + HD : (x + 1) * VSLICE]
            terms[slot, 16:17, :] = square_row

            @pl.when(slot != me)
            def _():
                send(3, terms.at[slot, pl.ds(0, 17)], gathered.at[me, pl.ds(0, 17)], (c, tp, x))

        return carry

    lax.fori_loop(0, CTX, head_block, 0)
    gathered[me, 0:17, :] = terms[me, 0:17, :]
    await_bytes(recv_sem.at[3], gathered.at[pl.ds(0, PLANE - 1), pl.ds(0, 17)])
    summed = jnp.sum(gathered[:, 0:16, :], axis=0)
    square_sum = jnp.sum(jnp.where(diagonal, jnp.sum(gathered[:, 16:17, :], axis=0), 0.0), axis=1, keepdims=True)
    logits = jnp.concatenate([summed[0:8], summed[8:16]], axis=1) * lax.rsqrt(square_sum / D + 1e-05)
    mine = pl.ds(pl.multiple_of(me * VSLICE, VSLICE), VSLICE)
    fin[:, mine] = logits

    def gather_logits(step, carry):
        send(4, fin.at[:, mine], fin.at[:, mine], plane_peer(step)[1])
        return carry

    half = lax.broadcasted_iota(jnp.int32, (B, HD), 1) < 64

    def merge(pairs):
        turned = pltpu.roll(pairs.reshape(-1, HD), 64, 1).reshape(pairs.shape)
        low = lax.broadcasted_iota(jnp.int32, pairs.shape, 2) < 64
        tops = jnp.where(low, pairs, turned)
        sums = jnp.where(low, turned, pairs)
        top = jnp.max(tops, axis=0)
        return top, jnp.sum(sums * jnp.exp(tops - top[None]), axis=0)

    top = jnp.max(logits, axis=1, keepdims=True)
    total = jnp.sum(jnp.exp(logits - top), axis=1, keepdims=True)
    zstat[tp] = jnp.where(half, top, total)

    def gather_zstat(step, carry):
        send(5, zstat.at[tp], zstat.at[tp], z_peer(step))
        return carry

    lax.fori_loop(1, TP, gather_zstat, 0)
    lax.fori_loop(1, PLANE, gather_logits, 0)
    await_bytes(recv_sem.at[5], zstat.at[pl.ds(0, TP - 1)])
    pstat[me] = jnp.where(half, *merge(zstat[...]))

    def gather_pstat(step, carry):
        send(6, pstat.at[me], pstat.at[me], plane_peer(step)[1])
        return carry

    lax.fori_loop(1, PLANE, gather_pstat, 0)
    await_bytes(recv_sem.at[6], pstat.at[pl.ds(0, PLANE - 1)])
    top, total = merge(pstat[...])
    shift = (top + jnp.log(total))[:, 0:1]
    await_bytes(recv_sem.at[4], fin.at[:, pl.ds(0, (PLANE - 1) * VSLICE)])
    out_ref[...] = fin[...] - shift

    await_bytes(send_sem.at[0], parts.at[pl.ds(0, PLANE - 1)])
    await_bytes(send_sem.at[1], att.at[pl.ds(0, PLANE - 1)])
    await_bytes(send_sem.at[2], proj.at[pl.ds(0, TP - 1)])
    await_bytes(send_sem.at[3], gathered.at[pl.ds(0, PLANE - 1), pl.ds(0, 17)])
    await_bytes(send_sem.at[4], fin.at[:, pl.ds(0, (PLANE - 1) * VSLICE)])
    await_bytes(send_sem.at[5], zstat.at[pl.ds(0, TP - 1)])
    await_bytes(send_sem.at[6], pstat.at[pl.ds(0, PLANE - 1)])


def shards(*args):
    vmem = pltpu.VMEM
    width = PLANE * VSLICE
    return pl.pallas_call(
        kernel,
        out_shape=jax.ShapeDtypeStruct((B, width), F32),
        in_specs=[pl.BlockSpec(memory_space=pl.ANY)] * 8,
        out_specs=pl.BlockSpec(memory_space=vmem),
        scratch_shapes=[
            pltpu.SMEM((B,), jnp.int32),
            vmem((B, GROUP * HD), BF16),
            vmem((B, SLOTS, HD), BF16),
            vmem((B, SLOTS, HD), BF16),
            vmem((GROUP * HD, FEAT), BF16),
            vmem((B, FEAT), BF16),
            vmem((FEAT,), F32),
            vmem((FEAT, width), BF16),
            vmem((GROUP * B, HD), F32),
            vmem((PLANE * 8, HD), F32),
            vmem((PLANE, 8, HD), F32),
            vmem((PLANE, 4, HD), F32),
            vmem((TP, B, FEAT), F32),
            vmem((PLANE, 24, HD), F32),
            vmem((PLANE, 24, HD), F32),
            vmem((B, width), F32),
            vmem((TP, B, HD), F32),
            vmem((PLANE, B, HD), F32),
            pltpu.SemaphoreType.DMA((8,)),
            pltpu.SemaphoreType.DMA((7,)),
            pltpu.SemaphoreType.DMA((7,)),
        ],
        compiler_params=pltpu.CompilerParams(
            collective_id=0, has_side_effects=True, vmem_limit_bytes=40 * 1024 * 1024
        ),
    )(*args)


def solution(mesh):
    return jax.shard_map(
        shards,
        mesh=mesh,
        in_specs=(
            P(),
            P(None, "tp"),
            P(None, ("ctx", "vocab"), "tp"),
            P(None, ("ctx", "vocab"), "tp"),
            P("tp", ("ctx", "vocab")),
            P(None, ("ctx", "vocab")),
            P(("ctx", "vocab")),
            P(("ctx", "vocab"), "tp"),
        ),
        out_specs=P(None, "tp"),
        check_vma=False,
    )
```

```python
import functools

import jax
import jax.numpy as jnp
from jax import lax
from jax.experimental import pallas as pl
from jax.experimental.pallas import tpu as pltpu
from jax.sharding import PartitionSpec as P

MESH = pl.DeviceIdType.MESH
CHIPS = sorted(((dy, dx) for dy in range(4) for dx in range(4)), key=lambda d: -(min(d[0], 4 - d[0]) + min(d[1], 4 - d[1])))
Z_STEPS = (4, 3, 5, 2, 6, 1, 7)
B = 8
D = 16384
HD = 128
GROUP = 16
CTX, TP, VOCAB = 8, 8, 4
PLANE = CTX * VOCAB
SLOTS = 512
FEAT = 512
VSLICE = 256
F32 = jnp.float32
BF16 = jnp.bfloat16

def kernel(
    len_hbm, q_hbm, k_hbm, v_hbm, w_hbm, res_hbm, gain_hbm, head_hbm,
    out_ref,
    lens, q, k, v, w, res, gain, head, qs,
    part, parts, att, proj, terms, gathered, fin, allstat,
    load_sem, send_sem, recv_sem,
):
    ctx, tp, voc = lax.axis_index("ctx"), lax.axis_index("tp"), lax.axis_index("vocab")
    me = ctx * VOCAB + voc

    chip_y, core = ctx // 2, lax.rem(ctx, 2)
    rows = [lax.rem(chip_y + d, 4) for d in range(4)]
    columns = [lax.rem(voc + d, 4) for d in range(4)]
    cores = [core, 1 - core]
    chips = [(rows[dy], columns[dx]) for dy, dx in CHIPS]
    plane = [
        ((y * 2 + c) * VOCAB + x, (y * 2 + c, tp, x))
        for (y, x), offset in zip(chips, CHIPS)
        for c in reversed(cores)
        if offset != (0, 0) or c is not core
    ]
    line = [(ctx, lax.rem(tp + d, TP), voc) for d in Z_STEPS]

    barrier = pltpu.get_barrier_semaphore()
    for device in line + [device for _, device in plane]:
        pl.semaphore_signal(barrier, inc=1, device_id=device, device_id_type=MESH)

    loads = [
        pltpu.make_async_copy(src, dst, load_sem.at[i])
        for i, (src, dst) in enumerate(
            [(q_hbm, q), (len_hbm, lens), (k_hbm, k), (v_hbm, v), (w_hbm, w), (res_hbm, res), (gain_hbm, gain), (head_hbm, head)]
        )
    ]
    for load in loads:
        load.start()

    def send(stage, src, dst, device):
        pltpu.make_async_remote_copy(
            src_ref=src, dst_ref=dst, send_sem=send_sem.at[stage], recv_sem=recv_sem.at[stage],
            device_id=device, device_id_type=MESH,
        ).start()

    def await_bytes(sem, like):
        pltpu.make_async_copy(like, like, sem).wait()

    loads[0].wait()
    for h in range(GROUP):
        qs[pl.ds(h * B, B), :] = q[:, h * HD : (h + 1) * HD].astype(F32)
    loads[1].wait()
    loads[2].wait()
    loads[3].wait()
    position = me * SLOTS + lax.broadcasted_iota(jnp.int32, (GROUP, SLOTS), 1)
    lane = lax.broadcasted_iota(jnp.int32, (GROUP, HD), 1)
    for b in range(B):
        query = qs[pl.ds(b, GROUP, stride=B), :].astype(BF16)
        scores = lax.dot_general(query, k[b], (((1,), (1,)), ((), ())), preferred_element_type=F32) * HD ** (-0.5)
        valid = position < lens[b]
        masked = jnp.where(valid, scores, -1e30)
        peak = jnp.max(masked, axis=1, keepdims=True)
        expo = jnp.where(valid, jnp.exp(masked - peak), 0.0)
        total = jnp.sum(expo, axis=1, keepdims=True)
        mixed = jnp.dot(expo.astype(BF16), v[b], preferred_element_type=F32)
        row = (b // 4) * 8 + b % 4
        part[pl.ds(row, GROUP, stride=16), :] = mixed
        part[pl.ds(row + 4, GROUP, stride=16), :] = jnp.where(lane < 64, peak, total)

    pl.semaphore_wait(barrier, PLANE - 1 + TP - 1)

    for slot, device in plane:
        send(0, part.at[pl.ds(pl.multiple_of(slot * 8, 8), 8), :], parts.at[me], device)
    parts[me] = part[pl.ds(pl.multiple_of(me * 8, 8), 8), :]
    await_bytes(recv_sem.at[0], parts.at[pl.ds(0, PLANE - 1)])

    stats = parts[:, 4:8, :]
    swapped = pltpu.roll(stats.reshape(PLANE * 4, HD), 64, 1).reshape(PLANE, 4, HD)
    low = lax.broadcasted_iota(jnp.int32, (PLANE, 4, HD), 2) < 64
    peaks = jnp.where(low, stats, swapped)
    totals = jnp.where(low, swapped, stats)
    top = jnp.max(peaks, axis=0, keepdims=True)
    factor = jnp.exp(peaks - top)
    total = jnp.sum(totals * factor, axis=0)
    attended = jnp.sum(parts[:, 0:4, :] * factor, axis=0) / total
    att[me] = attended

    for _, device in plane:
        send(1, att.at[me], att.at[me], device)
    loads[4].wait()
    await_bytes(recv_sem.at[1], att.at[pl.ds(0, PLANE - 1)])

    heads = [
        jnp.concatenate([att[2 * h], att[2 * h + 1]], axis=0).astype(BF16) for h in range(GROUP)
    ]
    proj[tp] = jnp.dot(jnp.concatenate(heads, axis=1), w[...], preferred_element_type=F32)

    for device in line:
        send(2, proj.at[tp], proj.at[tp], device)
    loads[5].wait()
    loads[6].wait()
    loads[7].wait()
    await_bytes(recv_sem.at[2], proj.at[pl.ds(0, TP - 1)])

    hidden = res[...].astype(F32) + jnp.sum(proj[...], axis=0)
    diagonal = lax.broadcasted_iota(jnp.int32, (B, HD), 0) == lax.broadcasted_iota(jnp.int32, (B, HD), 1)
    squares = jnp.sum(hidden * hidden, axis=1, keepdims=True)
    square_row = jnp.sum(jnp.where(diagonal, squares, 0.0), axis=0, keepdims=True)
    scaled = (hidden * gain[...].reshape(1, FEAT)).astype(BF16)

    for (y, x), offset in zip(chips, CHIPS):
        pair = y * VOCAB + x
        width = 2 * VSLICE
        block = jnp.dot(scaled, head[:, pl.ds(pl.multiple_of(pair * width, width), width)], preferred_element_type=F32)
        for c in range(2):
            slot = pair * 2 + c
            terms[slot, 0:8, :] = block[:, c * VSLICE : c * VSLICE + HD]
            terms[slot, 8:16, :] = block[:, c * VSLICE + HD : (c + 1) * VSLICE]
            terms[slot, 16:17, :] = square_row
        for c in reversed(cores):
            if offset != (0, 0) or c is not core:
                send(3, terms.at[pair * 2 + c, pl.ds(0, 17)], gathered.at[me, pl.ds(0, 17)], (y * 2 + c, tp, x))

    slice_index = (chip_y * VOCAB + voc) * 2 + core
    gathered[me, 0:17, :] = terms[slice_index, 0:17, :]

    await_bytes(recv_sem.at[3], gathered.at[pl.ds(0, PLANE - 1), pl.ds(0, 17)])

    summed = jnp.sum(gathered[:, 0:16, :], axis=0)
    square_sum = jnp.sum(jnp.where(diagonal, jnp.sum(gathered[:, 16:17, :], axis=0), 0.0), axis=1, keepdims=True)
    logits = jnp.concatenate([summed[0:8], summed[8:16]], axis=1) * lax.rsqrt(square_sum / D + 1e-05)
    mine = pl.ds(pl.multiple_of(slice_index * VSLICE, VSLICE), VSLICE)
    fin[:, mine] = logits

    paired = lax.rem(lax.broadcasted_iota(jnp.int32, (B, HD), 1), 64) == lax.broadcasted_iota(jnp.int32, (B, HD), 0)
    half = lax.broadcasted_iota(jnp.int32, (B, HD), 1) < 64

    def merge(pairs):
        turned = pltpu.roll(pairs.reshape(-1, HD), 64, 1).reshape(pairs.shape)
        low = lax.broadcasted_iota(jnp.int32, pairs.shape, 2) < 64
        tops = jnp.where(low, pairs, turned)
        sums = jnp.where(low, turned, pairs)
        top = jnp.max(tops, axis=0)
        return top, jnp.sum(sums * jnp.exp(tops - top[None]), axis=0)

    top = jnp.max(logits, axis=1, keepdims=True)
    total = jnp.sum(jnp.exp(logits - top), axis=1, keepdims=True)
    here = me * TP + tp
    allstat[here] = jnp.sum(jnp.where(paired, jnp.where(half, top, total), 0.0), axis=0, keepdims=True)

    def gather_stat(step, carry):
        t = lax.rem(tp + 4 + (1 - 2 * lax.rem(step, 2)) * ((step + 1) // 2), TP)
        for _, (c, _, x) in plane:
            send(5, allstat.at[here], allstat.at[here], (c, t, x))
        return carry
    for _, device in plane:
        send(4, fin.at[:, mine], fin.at[:, mine], device)
    lax.fori_loop(0, 8, gather_stat, 0)
    for t_line in line:
        send(5, allstat.at[here], allstat.at[here], t_line)

    await_bytes(recv_sem.at[5], allstat.at[pl.ds(0, PLANE * TP - 1)])

    pairs = allstat[...]
    best = jnp.max(pairs, axis=0, keepdims=True)
    turned = pltpu.roll(pairs.reshape(PLANE * TP, HD), 64, 1).reshape(pairs.shape)
    sums = jnp.sum(turned * jnp.exp(jnp.minimum(pairs - best, 0.0)), axis=0, keepdims=True)
    shift = jnp.sum(jnp.where(diagonal, (best + jnp.log(sums)).reshape(1, HD), 0.0), axis=1, keepdims=True)
    await_bytes(recv_sem.at[4], fin.at[:, pl.ds(0, (PLANE - 1) * VSLICE)])
    out_ref[...] = fin[...] - shift

    await_bytes(send_sem.at[0], parts.at[pl.ds(0, PLANE - 1)])
    await_bytes(send_sem.at[1], att.at[pl.ds(0, PLANE - 1)])
    await_bytes(send_sem.at[2], proj.at[pl.ds(0, TP - 1)])
    await_bytes(send_sem.at[3], gathered.at[pl.ds(0, PLANE - 1), pl.ds(0, 17)])
    await_bytes(send_sem.at[4], fin.at[:, pl.ds(0, (PLANE - 1) * VSLICE)])
    await_bytes(send_sem.at[5], allstat.at[pl.ds(0, PLANE * TP - 1)])

def shards(*args):
    vmem = pltpu.VMEM
    width = PLANE * VSLICE
    return pl.pallas_call(
        kernel,
        out_shape=pltpu.VMEM((B, width), F32),
        in_specs=[pl.BlockSpec(memory_space=pl.ANY)] * 8,
        out_specs=pl.BlockSpec(memory_space=vmem),
        scratch_shapes=[
            pltpu.SMEM((B,), jnp.int32),
            vmem((B, GROUP * HD), BF16),
            vmem((B, SLOTS, HD), BF16),
            vmem((B, SLOTS, HD), BF16),
            vmem((GROUP * HD, FEAT), BF16),
            vmem((B, FEAT), BF16),
            vmem((FEAT,), F32),
            vmem((FEAT, width), BF16),
            vmem((GROUP * B, HD), F32),
            vmem((PLANE * 8, HD), F32),
            vmem((PLANE, 8, HD), F32),
            vmem((PLANE, 4, HD), F32),
            vmem((TP, B, FEAT), F32),
            vmem((PLANE, 24, HD), F32),
            vmem((PLANE, 24, HD), F32),
            vmem((B, width), F32),
            vmem((PLANE * TP, 1, HD), F32),
            pltpu.SemaphoreType.DMA((8,)),
            pltpu.SemaphoreType.DMA((7,)),
            pltpu.SemaphoreType.DMA((7,)),
        ],
        compiler_params=pltpu.CompilerParams(
            collective_id=0, has_side_effects=True, vmem_limit_bytes=40 * 1024 * 1024
        ),
    )(*[pltpu.with_memory_space_constraint(a, pltpu.HBM) for a in args])

def solution(mesh):
    return jax.shard_map(
        shards,
        mesh=mesh,
        in_specs=(
            P(),
            P(None, "tp"),
            P(None, ("ctx", "vocab"), "tp"),
            P(None, ("ctx", "vocab"), "tp"),
            P("tp", ("ctx", "vocab")),
            P(None, ("ctx", "vocab")),
            P(("ctx", "vocab")),
            P(("ctx", "vocab"), "tp"),
        ),
        out_specs=P(None, "tp"),
        check_vma=False,
    )
```

```python
import functools

import jax
import jax.numpy as jnp
from jax import lax
from jax.experimental import pallas as pl
from jax.experimental.pallas import tpu as pltpu
from jax.sharding import PartitionSpec as P

MESH = pl.DeviceIdType.MESH
CHIPS = sorted(((dy, dx) for dy in range(4) for dx in range(4)), key=lambda d: -(min(d[0], 4 - d[0]) + min(d[1], 4 - d[1])))
Z_STEPS = (4, 3, 5, 2, 6, 1, 7)
B = 8
D = 16384
HD = 128
GROUP = 16
CTX, TP, VOCAB = 8, 8, 4
PLANE = CTX * VOCAB
SLOTS = 512
FEAT = 512
VSLICE = 256
F32 = jnp.float32
BF16 = jnp.bfloat16

def kernel(
    len_hbm, q_hbm, k_hbm, v_hbm, w_hbm, res_hbm, gain_hbm, head_hbm,
    out_ref,
    lens, q, k, v, w, res, gain, head, qs,
    part, parts, att, proj, terms, gathered, fin, allstat, rowlike,
    load_sem, send_sem, recv_sem,
):
    ctx, tp, voc = lax.axis_index("ctx"), lax.axis_index("tp"), lax.axis_index("vocab")
    me = ctx * VOCAB + voc

    chip_y, core = ctx // 2, lax.rem(ctx, 2)
    rows = [lax.rem(chip_y + d, 4) for d in range(4)]
    columns = [lax.rem(voc + d, 4) for d in range(4)]
    cores = [core, 1 - core]
    chips = [(rows[dy], columns[dx]) for dy, dx in CHIPS]
    plane = [
        ((y * 2 + c) * VOCAB + x, (y * 2 + c, tp, x))
        for (y, x), offset in zip(chips, CHIPS)
        for c in reversed(cores)
        if offset != (0, 0) or c is not core
    ]
    line = [(ctx, lax.rem(tp + d, TP), voc) for d in Z_STEPS]

    barrier = pltpu.get_barrier_semaphore()
    for device in [device for _, device in plane] + line:
        pl.semaphore_signal(barrier, inc=1, device_id=device, device_id_type=MESH)

    loads = [
        pltpu.make_async_copy(src, dst, load_sem.at[i])
        for i, (src, dst) in enumerate(
            [(q_hbm, q), (len_hbm, lens), (k_hbm, k), (v_hbm, v), (w_hbm, w), (res_hbm, res), (gain_hbm, gain), (head_hbm, head)]
        )
    ]
    for load in loads:
        load.start()

    def send(stage, src, dst, device):
        pltpu.make_async_remote_copy(
            src_ref=src, dst_ref=dst, send_sem=send_sem.at[stage], recv_sem=recv_sem.at[stage],
            device_id=device, device_id_type=MESH,
        ).start()

    def await_bytes(sem, like):
        pltpu.make_async_copy(like, like, sem).wait()

    loads[0].wait()
    for h in range(GROUP):
        qs[pl.ds(h * B, B), :] = q[:, h * HD : (h + 1) * HD].astype(F32)
    loads[1].wait()
    loads[2].wait()
    position = me * SLOTS + lax.broadcasted_iota(jnp.int32, (GROUP, SLOTS), 1)
    lane = lax.broadcasted_iota(jnp.int32, (GROUP, HD), 1)
    scores = jnp.concatenate(
        [
            lax.dot_general(
                qs[pl.ds(b, GROUP, stride=B), :].astype(BF16), k[b], (((1,), (1,)), ((), ())), preferred_element_type=F32
            )
            for b in range(B)
        ],
        axis=0,
    ) * HD ** (-0.5)
    valid = jnp.concatenate([position < lens[b] for b in range(B)], axis=0)
    masked = jnp.where(valid, scores, -1e30)
    peak = jnp.max(masked, axis=1, keepdims=True)
    expo = jnp.where(valid, jnp.exp(masked - peak), 0.0)
    total = jnp.sum(expo, axis=1, keepdims=True)
    weights = expo.astype(BF16)
    loads[3].wait()
    for b in range(B):
        mine = slice(b * GROUP, (b + 1) * GROUP)
        at = (b // 4) * 8 + b % 4
        part[pl.ds(at, GROUP, stride=16), :] = jnp.dot(weights[mine], v[b], preferred_element_type=F32)
        part[pl.ds(at + 4, GROUP, stride=16), :] = jnp.where(lane < 64, peak[mine], total[mine])

    pl.semaphore_wait(barrier, PLANE - 1 + TP - 1)

    for slot, device in plane:
        send(0, part.at[pl.ds(pl.multiple_of(slot * 8, 8), 8), :], parts.at[me], device)
    parts[me] = part[pl.ds(pl.multiple_of(me * 8, 8), 8), :]
    await_bytes(recv_sem.at[0], parts.at[pl.ds(0, PLANE - 1)])

    stats = parts[:, 4:8, :]
    swapped = pltpu.roll(stats.reshape(PLANE * 4, HD), 64, 1).reshape(PLANE, 4, HD)
    low = lax.broadcasted_iota(jnp.int32, (PLANE, 4, HD), 2) < 64
    peaks = jnp.where(low, stats, swapped)
    totals = jnp.where(low, swapped, stats)
    top = jnp.max(peaks, axis=0, keepdims=True)
    factor = jnp.exp(peaks - top)
    total = jnp.sum(totals * factor, axis=0)
    attended = jnp.sum(parts[:, 0:4, :] * factor, axis=0) / total
    att[me] = attended

    for _, device in plane:
        send(1, att.at[me], att.at[me], device)
    loads[4].wait()
    await_bytes(recv_sem.at[1], att.at[pl.ds(0, PLANE - 1)])

    heads = [
        jnp.concatenate([att[2 * h], att[2 * h + 1]], axis=0).astype(BF16) for h in range(GROUP)
    ]
    proj[tp] = jnp.dot(jnp.concatenate(heads, axis=1), w[...], preferred_element_type=F32)

    for device in line:
        send(2, proj.at[tp], proj.at[tp], device)
    loads[5].wait()
    loads[6].wait()
    loads[7].wait()
    await_bytes(recv_sem.at[2], proj.at[pl.ds(0, TP - 1)])

    hidden = res[...].astype(F32) + jnp.sum(proj[...], axis=0)
    diagonal = lax.broadcasted_iota(jnp.int32, (B, HD), 0) == lax.broadcasted_iota(jnp.int32, (B, HD), 1)
    squares = jnp.sum(hidden * hidden, axis=1, keepdims=True)
    square_row = jnp.sum(jnp.where(diagonal, squares, 0.0), axis=0, keepdims=True)
    scaled = (hidden * gain[...].reshape(1, FEAT)).astype(BF16)

    def head_terms(y, x):
        width = 2 * VSLICE
        columns = pl.ds(pl.multiple_of((y * VOCAB + x) * width, width), width)
        return jnp.dot(scaled, head[:, columns], preferred_element_type=F32)

    def send_terms(block, y, x, offset):
        for c in range(2):
            slot = (y * VOCAB + x) * 2 + c
            terms[slot, 0:8, :] = block[:, c * VSLICE : c * VSLICE + HD]
            terms[slot, 8:16, :] = block[:, c * VSLICE + HD : (c + 1) * VSLICE]
            terms[slot, 16:17, :] = square_row
        for c in reversed(cores):
            if offset != (0, 0) or c is not core:
                slot = (y * VOCAB + x) * 2 + c
                send(3, terms.at[slot, pl.ds(0, 17)], gathered.at[me, pl.ds(0, 17)], (y * 2 + c, tp, x))

    ahead = []
    for (y, x), offset in zip(chips, CHIPS):
        ahead.append((head_terms(y, x), y, x, offset))
        if len(ahead) > 2:
            for _ in range(1):
                send_terms(*ahead.pop(0))
    for block in ahead:
        send_terms(*block)

    slice_index = (chip_y * VOCAB + voc) * 2 + core
    gathered[me, 0:17, :] = terms[slice_index, 0:17, :]

    await_bytes(recv_sem.at[3], gathered.at[pl.ds(0, PLANE - 1), pl.ds(0, 17)])

    summed = jnp.sum(gathered[:, 0:16, :], axis=0)
    square_sum = jnp.sum(jnp.where(diagonal, jnp.sum(gathered[:, 16:17, :], axis=0), 0.0), axis=1, keepdims=True)
    logits = jnp.concatenate([summed[0:8], summed[8:16]], axis=1) * lax.rsqrt(square_sum / D + 1e-05)
    mine = pl.ds(pl.multiple_of(slice_index * VSLICE, VSLICE), VSLICE)
    fin[:, mine] = logits

    top = jnp.max(logits, axis=1, keepdims=True)
    local = top + jnp.log(jnp.sum(jnp.exp(logits - top), axis=1, keepdims=True))
    allstat[me, pl.ds(tp, 1), :] = jnp.sum(jnp.where(diagonal, local, 0.0), axis=0, keepdims=True)

    def gather_stat(step, carry):
        t = lax.rem(tp + 4 + (1 - 2 * lax.rem(step, 2)) * ((step + 1) // 2), TP)
        for _, (c, _, x) in plane:
            send(5, allstat.at[me, pl.ds(tp, 1), :], allstat.at[me, pl.ds(tp, 1), :], (c, t, x))
        return carry
    for _, device in plane:
        send(4, fin.at[:, mine], fin.at[:, mine], device)
    lax.fori_loop(0, 8, gather_stat, 0)
    for t_line in line:
        send(5, allstat.at[me, pl.ds(tp, 1), :], allstat.at[me, pl.ds(tp, 1), :], t_line)

    await_bytes(recv_sem.at[5], rowlike.at[pl.ds(0, PLANE * TP - 1)])

    slices = allstat[...]
    best = jnp.max(jnp.max(slices, axis=0), axis=0, keepdims=True)
    sums = jnp.sum(jnp.sum(jnp.exp(slices - best[None]), axis=0), axis=0, keepdims=True)
    shift = jnp.sum(jnp.where(diagonal, (best + jnp.log(sums)).reshape(1, HD), 0.0), axis=1, keepdims=True)
    await_bytes(recv_sem.at[4], fin.at[:, pl.ds(0, (PLANE - 1) * VSLICE)])
    out_ref[...] = fin[...] - shift

    await_bytes(send_sem.at[0], parts.at[pl.ds(0, PLANE - 1)])
    await_bytes(send_sem.at[1], att.at[pl.ds(0, PLANE - 1)])
    await_bytes(send_sem.at[2], proj.at[pl.ds(0, TP - 1)])
    await_bytes(send_sem.at[3], gathered.at[pl.ds(0, PLANE - 1), pl.ds(0, 17)])
    await_bytes(send_sem.at[4], fin.at[:, pl.ds(0, (PLANE - 1) * VSLICE)])
    await_bytes(send_sem.at[5], rowlike.at[pl.ds(0, PLANE * TP - 1)])

def shards(*args):
    vmem = pltpu.VMEM
    width = PLANE * VSLICE
    return pl.pallas_call(
        kernel,
        out_shape=pltpu.VMEM((B, width), F32),
        in_specs=[pl.BlockSpec(memory_space=pl.ANY)] * 8,
        out_specs=pl.BlockSpec(memory_space=vmem),
        scratch_shapes=[
            pltpu.SMEM((B,), jnp.int32),
            vmem((B, GROUP * HD), BF16),
            vmem((B, SLOTS, HD), BF16),
            vmem((B, SLOTS, HD), BF16),
            vmem((GROUP * HD, FEAT), BF16),
            vmem((B, FEAT), BF16),
            vmem((FEAT,), F32),
            vmem((FEAT, width), BF16),
            vmem((GROUP * B, HD), F32),
            vmem((PLANE * 8, HD), F32),
            vmem((PLANE, 8, HD), F32),
            vmem((PLANE, 4, HD), F32),
            vmem((TP, B, FEAT), F32),
            vmem((PLANE, 24, HD), F32),
            vmem((PLANE, 24, HD), F32),
            vmem((B, width), F32),
            vmem((PLANE, TP, HD), F32),
            vmem((PLANE * TP, 1, HD), F32),
            pltpu.SemaphoreType.DMA((8,)),
            pltpu.SemaphoreType.DMA((7,)),
            pltpu.SemaphoreType.DMA((7,)),
        ],
        compiler_params=pltpu.CompilerParams(
            collective_id=0, has_side_effects=True, vmem_limit_bytes=40 * 1024 * 1024
        ),
    )(*[pltpu.with_memory_space_constraint(a, pltpu.HBM) for a in args])

def solution(mesh):
    return jax.shard_map(
        shards,
        mesh=mesh,
        in_specs=(
            P(),
            P(None, "tp"),
            P(None, ("ctx", "vocab"), "tp"),
            P(None, ("ctx", "vocab"), "tp"),
            P("tp", ("ctx", "vocab")),
            P(None, ("ctx", "vocab")),
            P(("ctx", "vocab")),
            P(("ctx", "vocab"), "tp"),
        ),
        out_specs=P(None, "tp"),
        check_vma=False,
    )
```

```python
import functools

import jax
import jax.numpy as jnp
from jax import lax
from jax.experimental import pallas as pl
from jax.experimental.pallas import tpu as pltpu
from jax.sharding import PartitionSpec as P

MESH = pl.DeviceIdType.MESH
CHIPS = sorted(((dy, dx) for dy in range(4) for dx in range(4)), key=lambda d: -(min(d[0], 4 - d[0]) + min(d[1], 4 - d[1])))
Z_STEPS = (4, 3, 5, 2, 6, 1, 7)
B = 8
D = 16384
HD = 128
GROUP = 16
CTX, TP, VOCAB = 8, 8, 4
PLANE = CTX * VOCAB
SLOTS = 512
FEAT = 512
VSLICE = 256
F32 = jnp.float32
BF16 = jnp.bfloat16

def kernel(
    len_hbm, q_hbm, k_hbm, v_hbm, w_hbm, res_hbm, gain_hbm, head_hbm,
    out_ref,
    lens, q, k, v, w, res, gain, head, qs,
    part, parts, att, proj, terms, gathered, fin, allstat, rowlike,
    load_sem, send_sem, recv_sem,
):
    ctx, tp, voc = lax.axis_index("ctx"), lax.axis_index("tp"), lax.axis_index("vocab")

    chip_y, core = ctx // 2, lax.rem(ctx, 2)
    rows = [lax.rem(chip_y + d, 4) for d in range(4)]
    columns = [lax.rem(voc + d, 4) for d in range(4)]
    cores = [core, 1 - core]
    me = (chip_y * VOCAB + voc) * 2 + core
    chips = [(rows[dy], columns[dx]) for dy, dx in CHIPS]
    plane = [
        ((y * VOCAB + x) * 2 + c, (y * 2 + c, tp, x))
        for (y, x), offset in zip(chips, CHIPS)
        for c in reversed(cores)
        if offset != (0, 0) or c is not core
    ]
    line = [(ctx, lax.rem(tp + d, TP), voc) for d in Z_STEPS]

    barrier = pltpu.get_barrier_semaphore()
    for device in [device for _, device in plane] + line:
        pl.semaphore_signal(barrier, inc=1, device_id=device, device_id_type=MESH)

    loads = [
        pltpu.make_async_copy(src, dst, load_sem.at[i])
        for i, (src, dst) in enumerate(
            [(q_hbm, q), (len_hbm, lens), (k_hbm, k), (v_hbm, v), (w_hbm, w), (res_hbm, res), (gain_hbm, gain), (head_hbm, head)]
        )
    ]
    for load in loads:
        load.start()

    def send(stage, src, dst, device):
        pltpu.make_async_remote_copy(
            src_ref=src, dst_ref=dst, send_sem=send_sem.at[stage], recv_sem=recv_sem.at[stage],
            device_id=device, device_id_type=MESH,
        ).start()

    def await_bytes(sem, like):
        pltpu.make_async_copy(like, like, sem).wait()

    loads[0].wait()
    for h in range(GROUP):
        qs[pl.ds(h * B, B), :] = q[:, h * HD : (h + 1) * HD].astype(F32)
    loads[1].wait()
    loads[2].wait()
    position = (ctx * VOCAB + voc) * SLOTS + lax.broadcasted_iota(jnp.int32, (GROUP, SLOTS), 1)
    lane = lax.broadcasted_iota(jnp.int32, (GROUP, HD), 1)
    scores = jnp.concatenate(
        [
            lax.dot_general(
                qs[pl.ds(b, GROUP, stride=B), :].astype(BF16), k[b], (((1,), (1,)), ((), ())), preferred_element_type=F32
            )
            for b in range(B)
        ],
        axis=0,
    ) * HD ** (-0.5)
    valid = jnp.concatenate([position < lens[b] for b in range(B)], axis=0)
    masked = jnp.where(valid, scores, -1e30)
    peak = jnp.max(masked, axis=1, keepdims=True)
    expo = jnp.where(valid, jnp.exp(masked - peak), 0.0)
    total = jnp.sum(expo, axis=1, keepdims=True)
    weights = expo.astype(BF16)
    loads[3].wait()
    for b in range(B):
        mine = slice(b * GROUP, (b + 1) * GROUP)
        at = (b // 4) * 8 + b % 4
        part[pl.ds(at, GROUP, stride=16), :] = jnp.dot(weights[mine], v[b], preferred_element_type=F32)
        part[pl.ds(at + 4, GROUP, stride=16), :] = jnp.where(lane < 64, peak[mine], total[mine])

    pl.semaphore_wait(barrier, PLANE - 1 + TP - 1)

    for slot, device in plane:
        send(0, part.at[pl.ds(pl.multiple_of(slot * 8, 8), 8), :], parts.at[me], device)
    parts[me] = part[pl.ds(pl.multiple_of(me * 8, 8), 8), :]
    await_bytes(recv_sem.at[0], parts.at[pl.ds(0, PLANE - 1)])

    stats = parts[:, 4:8, :]
    swapped = pltpu.roll(stats.reshape(PLANE * 4, HD), 64, 1).reshape(PLANE, 4, HD)
    low = lax.broadcasted_iota(jnp.int32, (PLANE, 4, HD), 2) < 64
    peaks = jnp.where(low, stats, swapped)
    totals = jnp.where(low, swapped, stats)
    top = jnp.max(peaks, axis=0, keepdims=True)
    factor = jnp.exp(peaks - top)
    total = jnp.sum(totals * factor, axis=0)
    attended = jnp.sum(parts[:, 0:4, :] * factor, axis=0) / total
    att[me] = attended

    for _, device in plane:
        send(1, att.at[me], att.at[me], device)
    loads[4].wait()
    await_bytes(recv_sem.at[1], att.at[pl.ds(0, PLANE - 1)])

    heads = [
        jnp.concatenate([att[2 * h], att[2 * h + 1]], axis=0).astype(BF16) for h in range(GROUP)
    ]
    proj[tp] = jnp.dot(jnp.concatenate(heads, axis=1), w[...], preferred_element_type=F32)

    for device in line:
        send(2, proj.at[tp], proj.at[tp], device)
    loads[5].wait()
    loads[6].wait()
    loads[7].wait()
    await_bytes(recv_sem.at[2], proj.at[pl.ds(0, TP - 1)])

    hidden = res[...].astype(F32) + jnp.sum(proj[...], axis=0)
    diagonal = lax.broadcasted_iota(jnp.int32, (B, HD), 0) == lax.broadcasted_iota(jnp.int32, (B, HD), 1)
    squares = jnp.sum(hidden * hidden, axis=1, keepdims=True)
    square_row = jnp.sum(jnp.where(diagonal, squares, 0.0), axis=0, keepdims=True)
    scaled = (hidden * gain[...].reshape(1, FEAT)).astype(BF16)

    def head_terms(y, x):
        width = 2 * VSLICE
        columns = pl.ds(pl.multiple_of((y * VOCAB + x) * width, width), width)
        return jnp.dot(scaled, head[:, columns], preferred_element_type=F32)

    def send_terms(block, y, x, offset):
        for c in range(2):
            slot = (y * VOCAB + x) * 2 + c
            terms[slot, 0:8, :] = block[:, c * VSLICE : c * VSLICE + HD]
            terms[slot, 8:16, :] = block[:, c * VSLICE + HD : (c + 1) * VSLICE]
            terms[slot, 16:17, :] = square_row
        for c in reversed(cores):
            if offset != (0, 0) or c is not core:
                slot = (y * VOCAB + x) * 2 + c
                send(3, terms.at[slot, pl.ds(0, 17)], gathered.at[me, pl.ds(0, 17)], (y * 2 + c, tp, x))

    ahead = []
    for (y, x), offset in zip(chips, CHIPS):
        ahead.append((head_terms(y, x), y, x, offset))
        if len(ahead) > 2:
            for _ in range(1):
                send_terms(*ahead.pop(0))
    for block in ahead:
        send_terms(*block)

    gathered[me, 0:17, :] = terms[me, 0:17, :]

    await_bytes(recv_sem.at[3], gathered.at[pl.ds(0, PLANE - 1), pl.ds(0, 17)])

    summed = jnp.sum(gathered[:, 0:16, :], axis=0)
    square_sum = jnp.sum(jnp.where(diagonal, jnp.sum(gathered[:, 16:17, :], axis=0), 0.0), axis=1, keepdims=True)
    logits = jnp.concatenate([summed[0:8], summed[8:16]], axis=1) * lax.rsqrt(square_sum / D + 1e-05)
    mine = pl.ds(pl.multiple_of(me * VSLICE, VSLICE), VSLICE)
    fin[:, mine] = logits
    for _, device in plane:
        send(4, fin.at[:, mine], fin.at[:, mine], device)

    top = jnp.max(logits, axis=1, keepdims=True)
    local = top + jnp.log(jnp.sum(jnp.exp(logits - top), axis=1, keepdims=True))
    allstat[me, pl.ds(tp, 1), :] = jnp.sum(jnp.where(diagonal, local, 0.0), axis=0, keepdims=True)

    def gather_stat(step, carry):
        t = lax.rem(tp + 4 + (1 - 2 * lax.rem(step, 2)) * ((step + 1) // 2), TP)
        for _, (c, _, x) in plane:
            send(5, allstat.at[me, pl.ds(tp, 1), :], allstat.at[me, pl.ds(tp, 1), :], (c, t, x))
        return carry
    lax.fori_loop(0, 8, gather_stat, 0)
    for t_line in line:
        send(5, allstat.at[me, pl.ds(tp, 1), :], allstat.at[me, pl.ds(tp, 1), :], t_line)

    await_bytes(recv_sem.at[5], rowlike.at[pl.ds(0, PLANE * TP - 1)])

    slices = allstat[...]
    best = jnp.max(jnp.max(slices, axis=0), axis=0, keepdims=True)
    sums = jnp.sum(jnp.sum(jnp.exp(slices - best[None]), axis=0), axis=0, keepdims=True)
    shift = jnp.sum(jnp.where(diagonal, (best + jnp.log(sums)).reshape(1, HD), 0.0), axis=1, keepdims=True)
    await_bytes(recv_sem.at[4], fin.at[:, pl.ds(0, (PLANE - 1) * VSLICE)])
    out_ref[...] = fin[...] - shift

    await_bytes(send_sem.at[0], parts.at[pl.ds(0, PLANE - 1)])
    await_bytes(send_sem.at[1], att.at[pl.ds(0, PLANE - 1)])
    await_bytes(send_sem.at[2], proj.at[pl.ds(0, TP - 1)])
    await_bytes(send_sem.at[3], gathered.at[pl.ds(0, PLANE - 1), pl.ds(0, 17)])
    await_bytes(send_sem.at[4], fin.at[:, pl.ds(0, (PLANE - 1) * VSLICE)])
    await_bytes(send_sem.at[5], rowlike.at[pl.ds(0, PLANE * TP - 1)])

def shards(*args):
    vmem = pltpu.VMEM
    width = PLANE * VSLICE
    return pl.pallas_call(
        kernel,
        out_shape=pltpu.VMEM((B, width), F32),
        in_specs=[pl.BlockSpec(memory_space=pl.ANY)] * 8,
        out_specs=pl.BlockSpec(memory_space=vmem),
        scratch_shapes=[
            pltpu.SMEM((B,), jnp.int32),
            vmem((B, GROUP * HD), BF16),
            vmem((B, SLOTS, HD), BF16),
            vmem((B, SLOTS, HD), BF16),
            vmem((GROUP * HD, FEAT), BF16),
            vmem((B, FEAT), BF16),
            vmem((FEAT,), F32),
            vmem((FEAT, width), BF16),
            vmem((GROUP * B, HD), F32),
            vmem((PLANE * 8, HD), F32),
            vmem((PLANE, 8, HD), F32),
            vmem((PLANE, 4, HD), F32),
            vmem((TP, B, FEAT), F32),
            vmem((PLANE, 24, HD), F32),
            vmem((PLANE, 24, HD), F32),
            vmem((B, width), F32),
            vmem((PLANE, TP, HD), F32),
            vmem((PLANE * TP, 1, HD), F32),
            pltpu.SemaphoreType.DMA((8,)),
            pltpu.SemaphoreType.DMA((7,)),
            pltpu.SemaphoreType.DMA((7,)),
        ],
        compiler_params=pltpu.CompilerParams(
            collective_id=0, has_side_effects=True, vmem_limit_bytes=40 * 1024 * 1024
        ),
    )(*[pltpu.with_memory_space_constraint(a, pltpu.HBM) for a in args])

def solution(mesh):
    return jax.shard_map(
        shards,
        mesh=mesh,
        in_specs=(
            P(),
            P(None, "tp"),
            P(None, ("ctx", "vocab"), "tp"),
            P(None, ("ctx", "vocab"), "tp"),
            P("tp", ("ctx", "vocab")),
            P(None, ("ctx", "vocab")),
            P(("ctx", "vocab")),
            P(("ctx", "vocab"), "tp"),
        ),
        out_specs=P(None, "tp"),
        check_vma=False,
    )
```

```python
import functools

import jax
import jax.numpy as jnp
from jax import lax
from jax.experimental import pallas as pl
from jax.experimental.pallas import tpu as pltpu
from jax.sharding import PartitionSpec as P

MESH = pl.DeviceIdType.MESH
CHIPS = sorted(((dy, dx) for dy in range(4) for dx in range(4)), key=lambda d: -(min(d[0], 4 - d[0]) + min(d[1], 4 - d[1])))
Z_STEPS = (4, 3, 5, 2, 6, 1, 7)
B = 8
D = 16384
HD = 128
GROUP = 16
CTX, TP, VOCAB = 8, 8, 4
PLANE = CTX * VOCAB
SLOTS = 512
FEAT = 512
VSLICE = 256
F32 = jnp.float32
BF16 = jnp.bfloat16

def kernel(
    len_hbm, q_hbm, k_hbm, v_hbm, w_hbm, res_hbm, gain_hbm, head_hbm,
    out_ref,
    lens, q, k, v, w, res, gain, head, qs,
    part, parts, att, proj, terms, gathered, fin, allstat, rowlike,
    load_sem, send_sem, recv_sem,
):
    ctx, tp, voc = lax.axis_index("ctx"), lax.axis_index("tp"), lax.axis_index("vocab")

    chip_y, core = ctx // 2, lax.rem(ctx, 2)
    rows = [lax.rem(chip_y + d, 4) for d in range(4)]
    columns = [lax.rem(voc + d, 4) for d in range(4)]
    cores = [core, 1 - core]
    me = (chip_y * VOCAB + voc) * 2 + core
    chips = [(rows[dy], columns[dx]) for dy, dx in CHIPS]
    plane = [
        ((y * VOCAB + x) * 2 + c, (y * 2 + c, tp, x))
        for (y, x), offset in zip(chips, CHIPS)
        for c in reversed(cores)
        if offset != (0, 0) or c is not core
    ]
    line = [(ctx, lax.rem(tp + d, TP), voc) for d in Z_STEPS]

    barrier = pltpu.get_barrier_semaphore()
    for device in line[:3] + [device for _, device in plane] + line[3:]:
        pl.semaphore_signal(barrier, inc=1, device_id=device, device_id_type=MESH)

    loads = [
        pltpu.make_async_copy(src, dst, load_sem.at[i])
        for i, (src, dst) in enumerate(
            [(q_hbm, q), (len_hbm, lens), (k_hbm, k), (v_hbm, v), (w_hbm, w), (res_hbm, res), (gain_hbm, gain), (head_hbm, head)]
        )
    ]
    for load in loads:
        load.start()

    def send(stage, src, dst, device):
        pltpu.make_async_remote_copy(
            src_ref=src, dst_ref=dst, send_sem=send_sem.at[stage], recv_sem=recv_sem.at[stage],
            device_id=device, device_id_type=MESH,
        ).start()

    def await_bytes(sem, like):
        pltpu.make_async_copy(like, like, sem).wait()

    loads[0].wait()
    for h in range(GROUP):
        qs[pl.ds(h * B, B), :] = q[:, h * HD : (h + 1) * HD].astype(F32)
    loads[1].wait()
    loads[2].wait()
    position = (ctx * VOCAB + voc) * SLOTS + lax.broadcasted_iota(jnp.int32, (GROUP, SLOTS), 1)
    lane = lax.broadcasted_iota(jnp.int32, (GROUP, HD), 1)
    scores = jnp.concatenate(
        [
            lax.dot_general(
                qs[pl.ds(b, GROUP, stride=B), :].astype(BF16), k[b], (((1,), (1,)), ((), ())), preferred_element_type=F32
            )
            for b in range(B)
        ],
        axis=0,
    ) * HD ** (-0.5)
    valid = jnp.concatenate([position < lens[b] for b in range(B)], axis=0)
    masked = jnp.where(valid, scores, -1e30)
    peak = jnp.max(masked, axis=1, keepdims=True)
    expo = jnp.where(valid, jnp.exp(masked - peak), 0.0)
    total = jnp.sum(expo, axis=1, keepdims=True)
    weights = expo.astype(BF16)
    live = total > 0.0
    inverse = jnp.where(live, 1.0 / jnp.where(live, total, 1.0), 0.0)
    level = jnp.where(live, peak + jnp.log(jnp.where(live, total, 1.0)), -1e30)
    loads[3].wait()
    for b in range(B):
        mine = slice(b * GROUP, (b + 1) * GROUP)
        at = (b // 4) * 8 + b % 4
        part[pl.ds(at, GROUP, stride=16), :] = jnp.dot(weights[mine], v[b], preferred_element_type=F32) * inverse[mine]
        if b % 2:
            before = slice((b - 1) * GROUP, b * GROUP)
            part[pl.ds((b // 4) * 8 + 4 + (b % 4) // 2, GROUP, stride=16), :] = jnp.where(lane < 64, level[before], level[mine])

    pl.semaphore_wait(barrier, PLANE - 1 + TP - 1)

    for slot, device in plane:
        send(0, part.at[pl.ds(pl.multiple_of(slot * 8, 8), 6), :], parts.at[me, pl.ds(0, 6)], device)
    parts[me] = part[pl.ds(pl.multiple_of(me * 8, 8), 8), :]
    await_bytes(recv_sem.at[0], parts.at[pl.ds(0, PLANE - 1), pl.ds(0, 6)])

    first = lax.broadcasted_iota(jnp.int32, (PLANE, 4, HD), 1)
    pairs = jnp.where(first < 2, parts[:, 4:5, :], parts[:, 5:6, :])
    turned = pltpu.roll(pairs.reshape(PLANE * 4, HD), 64, 1).reshape(PLANE, 4, HD)
    low = lax.broadcasted_iota(jnp.int32, (PLANE, 4, HD), 2) < 64
    levels = jnp.where(low == (lax.rem(first, 2) == 0), pairs, turned)
    factor = jnp.exp(levels - jnp.max(levels, axis=0, keepdims=True))
    attended = jnp.sum(parts[:, 0:4, :] * factor, axis=0) / jnp.sum(factor, axis=0)
    att[me] = attended

    for _, device in plane:
        send(1, att.at[me], att.at[me], device)
    loads[4].wait()
    await_bytes(recv_sem.at[1], att.at[pl.ds(0, PLANE - 1)])

    heads = [
        jnp.concatenate([att[2 * h], att[2 * h + 1]], axis=0).astype(BF16) for h in range(GROUP)
    ]
    proj[tp] = jnp.dot(jnp.concatenate(heads, axis=1), w[...], preferred_element_type=F32)

    for device in line:
        send(2, proj.at[tp], proj.at[tp], device)
    loads[5].wait()
    loads[6].wait()
    loads[7].wait()
    await_bytes(recv_sem.at[2], proj.at[pl.ds(0, TP - 1)])

    hidden = res[...].astype(F32) + jnp.sum(proj[...], axis=0)
    diagonal = lax.broadcasted_iota(jnp.int32, (B, HD), 0) == lax.broadcasted_iota(jnp.int32, (B, HD), 1)
    squares = jnp.sum(hidden * hidden, axis=1, keepdims=True)
    square_row = jnp.sum(jnp.where(diagonal, squares, 0.0), axis=0, keepdims=True)
    scaled = (hidden * gain[...].reshape(1, FEAT)).astype(BF16)

    def head_terms(y, x):
        width = 2 * VSLICE
        columns = pl.ds(pl.multiple_of((y * VOCAB + x) * width, width), width)
        return jnp.dot(scaled, head[:, columns], preferred_element_type=F32)

    def send_terms(block, y, x, offset):
        for c in range(2):
            slot = (y * VOCAB + x) * 2 + c
            terms[slot, 0:8, :] = block[:, c * VSLICE : c * VSLICE + HD]
            terms[slot, 8:16, :] = block[:, c * VSLICE + HD : (c + 1) * VSLICE]
            terms[slot, 16:17, :] = square_row
        for c in reversed(cores):
            if offset != (0, 0) or c is not core:
                slot = (y * VOCAB + x) * 2 + c
                send(3, terms.at[slot, pl.ds(0, 17)], gathered.at[me, pl.ds(0, 17)], (y * 2 + c, tp, x))

    ahead = []
    for (y, x), offset in zip(chips, CHIPS):
        ahead.append((head_terms(y, x), y, x, offset))
        if len(ahead) > 2:
            for _ in range(1):
                send_terms(*ahead.pop(0))
    for block in ahead:
        send_terms(*block)

    gathered[me, 0:17, :] = terms[me, 0:17, :]

    await_bytes(recv_sem.at[3], gathered.at[pl.ds(0, PLANE - 1), pl.ds(0, 17)])

    summed = jnp.sum(gathered[:, 0:16, :], axis=0)
    square_sum = jnp.sum(jnp.where(diagonal, jnp.sum(gathered[:, 16:17, :], axis=0), 0.0), axis=1, keepdims=True)
    logits = jnp.concatenate([summed[0:8], summed[8:16]], axis=1) * lax.rsqrt(square_sum / D + 1e-05)
    mine = pl.ds(pl.multiple_of(me * VSLICE, VSLICE), VSLICE)
    fin[:, mine] = logits
    for _, device in plane:
        send(4, fin.at[:, mine], fin.at[:, mine], device)

    top = jnp.max(logits, axis=1, keepdims=True)
    local = top + jnp.log(jnp.sum(jnp.exp(logits - top), axis=1, keepdims=True))
    allstat[me, pl.ds(tp, 1), :] = jnp.sum(jnp.where(diagonal, local, 0.0), axis=0, keepdims=True)

    def gather_stat(step, carry):
        t = lax.rem(tp + 4 + (1 - 2 * lax.rem(step, 2)) * ((step + 1) // 2), TP)
        for _, (c, _, x) in plane:
            send(5, allstat.at[me, pl.ds(tp, 1), :], allstat.at[me, pl.ds(tp, 1), :], (c, t, x))
        return carry
    lax.fori_loop(0, 8, gather_stat, 0)
    for t_line in line:
        send(5, allstat.at[me, pl.ds(tp, 1), :], allstat.at[me, pl.ds(tp, 1), :], t_line)

    await_bytes(recv_sem.at[5], rowlike.at[pl.ds(0, PLANE * TP - 1)])

    slices = allstat[...]
    best = jnp.max(jnp.max(slices, axis=0), axis=0, keepdims=True)
    sums = jnp.sum(jnp.sum(jnp.exp(slices - best[None]), axis=0), axis=0, keepdims=True)
    shift = jnp.sum(jnp.where(diagonal, (best + jnp.log(sums)).reshape(1, HD), 0.0), axis=1, keepdims=True)
    await_bytes(recv_sem.at[4], fin.at[:, pl.ds(0, (PLANE - 1) * VSLICE)])
    out_ref[...] = fin[...] - shift

    await_bytes(send_sem.at[0], parts.at[pl.ds(0, PLANE - 1), pl.ds(0, 6)])
    await_bytes(send_sem.at[1], att.at[pl.ds(0, PLANE - 1)])
    await_bytes(send_sem.at[2], proj.at[pl.ds(0, TP - 1)])
    await_bytes(send_sem.at[3], gathered.at[pl.ds(0, PLANE - 1), pl.ds(0, 17)])
    await_bytes(send_sem.at[4], fin.at[:, pl.ds(0, (PLANE - 1) * VSLICE)])
    await_bytes(send_sem.at[5], rowlike.at[pl.ds(0, PLANE * TP - 1)])

def shards(*args):
    vmem = pltpu.VMEM
    width = PLANE * VSLICE
    return pl.pallas_call(
        kernel,
        out_shape=pltpu.VMEM((B, width), F32),
        in_specs=[pl.BlockSpec(memory_space=pl.ANY)] * 8,
        out_specs=pl.BlockSpec(memory_space=vmem),
        scratch_shapes=[
            pltpu.SMEM((B,), jnp.int32),
            vmem((B, GROUP * HD), BF16),
            vmem((B, SLOTS, HD), BF16),
            vmem((B, SLOTS, HD), BF16),
            vmem((GROUP * HD, FEAT), BF16),
            vmem((B, FEAT), BF16),
            vmem((FEAT,), F32),
            vmem((FEAT, width), BF16),
            vmem((GROUP * B + B, HD), F32),
            vmem((PLANE * 8 + 16, HD), F32),
            vmem((PLANE, 8, HD), F32),
            vmem((PLANE, 4, HD), F32),
            vmem((TP, B, FEAT), F32),
            vmem((PLANE, 24, HD), F32),
            vmem((PLANE, 24, HD), F32),
            vmem((B, width), F32),
            vmem((PLANE, TP, HD), F32),
            vmem((PLANE * TP, 1, HD), F32),
            pltpu.SemaphoreType.DMA((8,)),
            pltpu.SemaphoreType.DMA((7,)),
            pltpu.SemaphoreType.DMA((7,)),
        ],
        compiler_params=pltpu.CompilerParams(
            collective_id=0, has_side_effects=True, vmem_limit_bytes=40 * 1024 * 1024
        ),
    )(*[pltpu.with_memory_space_constraint(a, pltpu.HBM) for a in args])

def solution(mesh):
    return jax.shard_map(
        shards,
        mesh=mesh,
        in_specs=(
            P(),
            P(None, "tp"),
            P(None, ("ctx", "vocab"), "tp"),
            P(None, ("ctx", "vocab"), "tp"),
            P("tp", ("ctx", "vocab")),
            P(None, ("ctx", "vocab")),
            P(("ctx", "vocab")),
            P(("ctx", "vocab"), "tp"),
        ),
        out_specs=P(None, "tp"),
        check_vma=False,
    )
```

```python
import functools

import jax
import jax.numpy as jnp
from jax import lax
from jax.experimental import pallas as pl
from jax.experimental.pallas import tpu as pltpu
from jax.sharding import PartitionSpec as P

MESH = pl.DeviceIdType.MESH
CHIPS = sorted(((dy, dx) for dy in range(4) for dx in range(4)), key=lambda d: -(min(d[0], 4 - d[0]) + min(d[1], 4 - d[1])))
Z_STEPS = (4, 3, 5, 2, 6, 1, 7)
B = 8
D = 16384
HD = 128
GROUP = 16
CTX, TP, VOCAB = 8, 8, 4
PLANE = CTX * VOCAB
SLOTS = 512
FEAT = 512
VSLICE = 256
F32 = jnp.float32
BF16 = jnp.bfloat16

def kernel(
    len_hbm, q_hbm, k_hbm, v_hbm, w_hbm, res_hbm, gain_hbm, head_hbm,
    out_ref,
    lens, q, k, v, w, res, gain, head, qs,
    part, parts, att, proj, terms, gathered, fin, allstat, rowlike,
    load_sem, send_sem, recv_sem,
):
    ctx, tp, voc = lax.axis_index("ctx"), lax.axis_index("tp"), lax.axis_index("vocab")

    chip_y, core = ctx // 2, lax.rem(ctx, 2)
    rows = [lax.rem(chip_y + d, 4) for d in range(4)]
    columns = [lax.rem(voc + d, 4) for d in range(4)]
    cores = [core, 1 - core]
    me = (chip_y * VOCAB + voc) * 2 + core
    chips = [(rows[dy], columns[dx]) for dy, dx in CHIPS]
    plane = [
        ((y * VOCAB + x) * 2 + c, (y * 2 + c, tp, x))
        for (y, x), offset in zip(chips, CHIPS)
        for c in cores
        if offset != (0, 0) or c is not core
    ]
    line = [(ctx, lax.rem(tp + d, TP), voc) for d in Z_STEPS]

    barrier = pltpu.get_barrier_semaphore()
    for device in line[:3] + [device for _, device in plane] + line[3:]:
        pl.semaphore_signal(barrier, inc=1, device_id=device, device_id_type=MESH)

    loads = [
        pltpu.make_async_copy(src, dst, load_sem.at[i])
        for i, (src, dst) in enumerate(
            [(q_hbm, q), (len_hbm, lens), (k_hbm, k), (v_hbm, v), (w_hbm, w), (res_hbm, res), (gain_hbm, gain), (head_hbm, head)]
        )
    ]
    for load in loads:
        load.start()

    def send(stage, src, dst, device):
        pltpu.make_async_remote_copy(
            src_ref=src, dst_ref=dst, send_sem=send_sem.at[stage], recv_sem=recv_sem.at[stage],
            device_id=device, device_id_type=MESH,
        ).start()

    def await_bytes(sem, like):
        pltpu.make_async_copy(like, like, sem).wait()

    loads[0].wait()
    for h in range(GROUP):
        qs[pl.ds(h * B, B), :] = q[:, h * HD : (h + 1) * HD].astype(F32)
    loads[1].wait()
    loads[2].wait()
    position = (ctx * VOCAB + voc) * SLOTS + lax.broadcasted_iota(jnp.int32, (GROUP, SLOTS), 1)
    lane = lax.broadcasted_iota(jnp.int32, (GROUP, HD), 1)
    scores = jnp.concatenate(
        [
            lax.dot_general(
                qs[pl.ds(b, GROUP, stride=B), :].astype(BF16), k[b], (((1,), (1,)), ((), ())), preferred_element_type=F32
            )
            for b in range(B)
        ],
        axis=0,
    ) * HD ** (-0.5)
    valid = jnp.concatenate([position < lens[b] for b in range(B)], axis=0)
    masked = jnp.where(valid, scores, -1e30)
    peak = jnp.max(masked, axis=1, keepdims=True)
    expo = jnp.where(valid, jnp.exp(masked - peak), 0.0)
    total = jnp.sum(expo, axis=1, keepdims=True)
    weights = expo.astype(BF16)
    live = total > 0.0
    inverse = jnp.where(live, 1.0 / jnp.where(live, total, 1.0), 0.0)
    level = jnp.where(live, peak + jnp.log(jnp.where(live, total, 1.0)), -1e30)
    loads[3].wait()
    for b in range(B):
        mine = slice(b * GROUP, (b + 1) * GROUP)
        at = (b // 4) * 8 + b % 4
        part[pl.ds(at, GROUP, stride=16), :] = jnp.dot(weights[mine], v[b], preferred_element_type=F32) * inverse[mine]
        if b % 2:
            before = slice((b - 1) * GROUP, b * GROUP)
            part[pl.ds((b // 4) * 8 + 4 + (b % 4) // 2, GROUP, stride=16), :] = jnp.where(lane < 64, level[before], level[mine])

    pl.semaphore_wait(barrier, PLANE - 1 + TP - 1)

    for slot, device in plane:
        send(0, part.at[pl.ds(pl.multiple_of(slot * 8, 8), 6), :], parts.at[me, pl.ds(0, 6)], device)
    parts[me] = part[pl.ds(pl.multiple_of(me * 8, 8), 8), :]
    await_bytes(recv_sem.at[0], parts.at[pl.ds(0, PLANE - 1), pl.ds(0, 6)])

    first = lax.broadcasted_iota(jnp.int32, (PLANE, 4, HD), 1)
    pairs = jnp.where(first < 2, parts[:, 4:5, :], parts[:, 5:6, :])
    turned = pltpu.roll(pairs.reshape(PLANE * 4, HD), 64, 1).reshape(PLANE, 4, HD)
    low = lax.broadcasted_iota(jnp.int32, (PLANE, 4, HD), 2) < 64
    levels = jnp.where(low == (lax.rem(first, 2) == 0), pairs, turned)
    factor = jnp.exp(levels - jnp.max(levels, axis=0, keepdims=True))
    attended = jnp.sum(parts[:, 0:4, :] * factor, axis=0) / jnp.sum(factor, axis=0)
    att[me] = attended

    for _, device in plane:
        send(1, att.at[me], att.at[me], device)
    loads[4].wait()
    await_bytes(recv_sem.at[1], att.at[pl.ds(0, PLANE - 1)])

    heads = [
        jnp.concatenate([att[2 * h], att[2 * h + 1]], axis=0).astype(BF16) for h in range(GROUP)
    ]
    proj[tp] = jnp.dot(jnp.concatenate(heads, axis=1), w[...], preferred_element_type=F32)

    for device in line:
        send(2, proj.at[tp], proj.at[tp], device)
    loads[5].wait()
    loads[6].wait()
    loads[7].wait()
    await_bytes(recv_sem.at[2], proj.at[pl.ds(0, TP - 1)])

    hidden = res[...].astype(F32) + jnp.sum(proj[...], axis=0)
    diagonal = lax.broadcasted_iota(jnp.int32, (B, HD), 0) == lax.broadcasted_iota(jnp.int32, (B, HD), 1)
    squares = jnp.sum(hidden * hidden, axis=1, keepdims=True)
    square_row = jnp.sum(jnp.where(diagonal, squares, 0.0), axis=0, keepdims=True)
    scaled = (hidden * gain[...].reshape(1, FEAT)).astype(BF16)

    def head_terms(y, x):
        width = 2 * VSLICE
        columns = pl.ds(pl.multiple_of((y * VOCAB + x) * width, width), width)
        return jnp.dot(scaled, head[:, columns], preferred_element_type=F32)

    def send_terms(block, y, x, offset):
        for c in range(2):
            slot = (y * VOCAB + x) * 2 + c
            terms[slot, 0:8, :] = block[:, c * VSLICE : c * VSLICE + HD]
            terms[slot, 8:16, :] = block[:, c * VSLICE + HD : (c + 1) * VSLICE]
            terms[slot, 16:17, :] = square_row
        for c in cores:
            if offset != (0, 0) or c is not core:
                slot = (y * VOCAB + x) * 2 + c
                send(3, terms.at[slot, pl.ds(0, 17)], gathered.at[me, pl.ds(0, 17)], (y * 2 + c, tp, x))

    ahead = []
    for (y, x), offset in zip(chips, CHIPS):
        ahead.append((head_terms(y, x), y, x, offset))
        if len(ahead) > 2:
            for _ in range(1):
                send_terms(*ahead.pop(0))
    for block in ahead:
        send_terms(*block)

    gathered[me, 0:17, :] = terms[me, 0:17, :]

    await_bytes(recv_sem.at[3], gathered.at[pl.ds(0, PLANE - 1), pl.ds(0, 17)])

    summed = jnp.sum(gathered[:, 0:16, :], axis=0)
    square_sum = jnp.sum(jnp.where(diagonal, jnp.sum(gathered[:, 16:17, :], axis=0), 0.0), axis=1, keepdims=True)
    logits = jnp.concatenate([summed[0:8], summed[8:16]], axis=1) * lax.rsqrt(square_sum / D + 1e-05)
    mine = pl.ds(pl.multiple_of(me * VSLICE, VSLICE), VSLICE)
    fin[:, mine] = logits
    for _, device in plane:
        send(4, fin.at[:, mine], fin.at[:, mine], device)

    top = jnp.max(logits, axis=1, keepdims=True)
    local = top + jnp.log(jnp.sum(jnp.exp(logits - top), axis=1, keepdims=True))
    allstat[me, pl.ds(tp, 1), :] = jnp.sum(jnp.where(diagonal, local, 0.0), axis=0, keepdims=True)

    def gather_stat(step, carry):
        t = lax.rem(tp + 4 + (1 - 2 * lax.rem(step, 2)) * ((step + 1) // 2), TP)
        for _, (c, _, x) in plane:
            send(5, allstat.at[me, pl.ds(tp, 1), :], allstat.at[me, pl.ds(tp, 1), :], (c, t, x))
        return carry
    lax.fori_loop(0, 8, gather_stat, 0)
    for t_line in line:
        send(5, allstat.at[me, pl.ds(tp, 1), :], allstat.at[me, pl.ds(tp, 1), :], t_line)

    await_bytes(recv_sem.at[5], rowlike.at[pl.ds(0, PLANE * TP - 1)])

    slices = allstat[...]
    best = jnp.max(jnp.max(slices, axis=0), axis=0, keepdims=True)
    sums = jnp.sum(jnp.sum(jnp.exp(slices - best[None]), axis=0), axis=0, keepdims=True)
    shift = jnp.sum(jnp.where(diagonal, (best + jnp.log(sums)).reshape(1, HD), 0.0), axis=1, keepdims=True)
    await_bytes(recv_sem.at[4], fin.at[:, pl.ds(0, (PLANE - 1) * VSLICE)])
    out_ref[...] = fin[...] - shift

    await_bytes(send_sem.at[0], parts.at[pl.ds(0, PLANE - 1), pl.ds(0, 6)])
    await_bytes(send_sem.at[1], att.at[pl.ds(0, PLANE - 1)])
    await_bytes(send_sem.at[2], proj.at[pl.ds(0, TP - 1)])
    await_bytes(send_sem.at[3], gathered.at[pl.ds(0, PLANE - 1), pl.ds(0, 17)])
    await_bytes(send_sem.at[4], fin.at[:, pl.ds(0, (PLANE - 1) * VSLICE)])
    await_bytes(send_sem.at[5], rowlike.at[pl.ds(0, PLANE * TP - 1)])

def shards(*args):
    vmem = pltpu.VMEM
    width = PLANE * VSLICE
    return pl.pallas_call(
        kernel,
        out_shape=pltpu.VMEM((B, width), F32),
        in_specs=[pl.BlockSpec(memory_space=pl.ANY)] * 8,
        out_specs=pl.BlockSpec(memory_space=vmem),
        scratch_shapes=[
            pltpu.SMEM((B,), jnp.int32),
            vmem((B, GROUP * HD), BF16),
            vmem((B, SLOTS, HD), BF16),
            vmem((B, SLOTS, HD), BF16),
            vmem((GROUP * HD, FEAT), BF16),
            vmem((B, FEAT), BF16),
            vmem((FEAT,), F32),
            vmem((FEAT, width), BF16),
            vmem((GROUP * B + B, HD), F32),
            vmem((PLANE * 8 + 16, HD), F32),
            vmem((PLANE, 8, HD), F32),
            vmem((PLANE, 4, HD), F32),
            vmem((TP, B, FEAT), F32),
            vmem((PLANE, 24, HD), F32),
            vmem((PLANE, 24, HD), F32),
            vmem((B, width), F32),
            vmem((PLANE, TP, HD), F32),
            vmem((PLANE * TP, 1, HD), F32),
            pltpu.SemaphoreType.DMA((8,)),
            pltpu.SemaphoreType.DMA((7,)),
            pltpu.SemaphoreType.DMA((7,)),
        ],
        compiler_params=pltpu.CompilerParams(
            collective_id=0, has_side_effects=True, vmem_limit_bytes=40 * 1024 * 1024
        ),
    )(*[pltpu.with_memory_space_constraint(a, pltpu.HBM) for a in args])

def solution(mesh):
    return jax.shard_map(
        shards,
        mesh=mesh,
        in_specs=(
            P(),
            P(None, "tp"),
            P(None, ("ctx", "vocab"), "tp"),
            P(None, ("ctx", "vocab"), "tp"),
            P("tp", ("ctx", "vocab")),
            P(None, ("ctx", "vocab")),
            P(("ctx", "vocab")),
            P(("ctx", "vocab"), "tp"),
        ),
        out_specs=P(None, "tp"),
        check_vma=False,
    )
```
